32 devices in a mesh: fsdp: 8 (over z, core), context: 2 (over y), tensor: 2 (over x).
Axes of the slice: x: 2, y: 2, z: 4, core: 2. Of those that a mesh axis runs over, the one named last changes fastest.
Arguments:
- block_input: bfloat16 [8192, 1024], P(('fsdp', 'context')), may hold values from -6 to 6
- cotangent: bfloat16 [8192, 1024], P(('fsdp', 'context')), may hold values from -6 to 6
- segments: int32 [8, 1024], P('fsdp'), may hold values from 0 to 2, as said below
- routes: int32 [8192, 8], P(('fsdp', 'context')), may hold values from 0 to 15, all different within a row; in each aligned block of 512 rows (0 to 511, 512 to 1023, ...) at most 320 rows name the same one
- attn_gain: bfloat16 [1024], P(('fsdp', 'context')), may hold values from 0.5 to 1.5
- query_weight: bfloat16 [1024, 1024], P(('fsdp', 'context'), 'tensor'), may hold values from -0.1875 to 0.1875
- key_weight: bfloat16 [1024, 512], P(('fsdp', 'context'), 'tensor'), may hold values from -0.1875 to 0.1875
- value_weight: bfloat16 [1024, 512], P(('fsdp', 'context'), 'tensor'), may hold values from -0.1875 to 0.1875
- out_weight: bfloat16 [1024, 1024], P('tensor', ('fsdp', 'context')), may hold values from -1.5 to 1.5
- ffn_gain: bfloat16 [1024], P(('fsdp', 'context')), may hold values from 0.5 to 1.5
- router_weight: bfloat16 [1024, 16], P(('fsdp', 'context')), may hold values from -0.09375 to 0.09375
- expert_gate: bfloat16 [16, 1024, 512], P('fsdp', None, 'tensor'), may hold values from -0.1875 to 0.1875
- expert_up: bfloat16 [16, 1024, 512], P('fsdp', None, 'tensor'), may hold values from -0.1875 to 0.1875
- expert_down: bfloat16 [16, 512, 1024], P('fsdp', 'tensor'), may hold values from -1 to 1
Outputs:
- output: bfloat16 [8192, 1024], P(('fsdp', 'context'))
- input_grad: float32 [8192, 1024], P(('fsdp', 'context'))
- grad_attn_gain: float32 [1024], P(('fsdp', 'context'))
- grad_query_weight: float32 [1024, 1024], P(('fsdp', 'context'), 'tensor')
- grad_key_weight: float32 [1024, 512], P(('fsdp', 'context'), 'tensor')
- grad_value_weight: float32 [1024, 512], P(('fsdp', 'context'), 'tensor')
- grad_out_weight: float32 [1024, 1024], P('tensor', ('fsdp', 'context'))
- grad_ffn_gain: float32 [1024], P(('fsdp', 'context'))
- grad_router_weight: float32 [1024, 16], P(('fsdp', 'context'))
- grad_expert_gate: float32 [16, 1024, 512], P('fsdp', 'context', 'tensor')
- grad_expert_up: float32 [16, 1024, 512], P('fsdp', 'context', 'tensor')
- grad_expert_down: float32 [16, 512, 1024], P('fsdp', 'tensor', 'context')
The draws below stay inside these ranges and needn't reach their ends.
Inputs may be any that keep to these rules, and one draw needn't show every extreme that they name: `segments`: each sequence holds three documents in order (segment numbers 0, 1, 2, never falling); the first and the last are shorter than 512 tokens, so the middle one runs from the first device's positions to the last device's. `routes`: each token names 8 different experts; among the 512 rows of one device no expert is named more than 320 times, and in every draw some expert is named exactly 320 times there.
All inputs are finite; a program needn't handle non-finite values.
Results may differ from the reference program's by a relative error of at most 0.035.
Values may be sent and summed in bfloat16 or wider, within the bound.
A program may use at most 192 MiB of HBM per device.

```python
import math
import jax
import jax.numpy as jnp
import numpy as np
from jax import lax

D = 1024
HEADS = 16
KV_HEADS = 8
HEAD_DIM = 64
FF = 512
TOPK = 8
SEQ_LEN = 1024
EXPERTS = 16
SEQS = 8
SEQ_DEV = 512
TOKENS = 8192
CAP = 320


def draw_segments(key, part):
    key = jax.random.fold_in(key, 11)
    first_key, last_key = jax.random.split(key)
    first_len = jax.random.randint(first_key, (SEQS, 1), SEQ_DEV // 4, SEQ_DEV).astype(jnp.int32)
    last_len = jax.random.randint(last_key, (SEQS, 1), SEQ_DEV // 4, SEQ_DEV).astype(jnp.int32)
    token_index = jnp.arange(SEQ_LEN, dtype=jnp.int32)[None, :]
    first_edge = (token_index >= first_len).astype(jnp.int32)
    last_edge = (token_index >= SEQ_LEN - last_len).astype(jnp.int32)
    return (first_edge + last_edge).astype(jnp.int32)


def steps_of(rng, extent, cuts, least, top_value):
    def one(position, shards_of):
        heights = jax.random.uniform(jax.random.fold_in(jax.random.fold_in(rng, 6), position), (shards_of,), jnp.float32, least / len(cuts), top_value / len(cuts))
        return jnp.repeat(jnp.exp(heights), extent[position] // shards_of).reshape((-1,) + (1,) * (len(extent) - position - 1))

    factor_of = one(*cuts[0])
    for cut in cuts[1:]:
        factor_of = factor_of * one(*cut)
    return factor_of


def assign_block(key, own, number, rows, count, top, bound, slope):
    order = jax.random.permutation(key, count)
    crowded, usual = load_shares(count, rows * top, bound, slope, True), load_shares(count, rows * top, bound, slope, False)
    places = jnp.arange(count)

    def named(tallies, turn):
        used = int((tallies > 0).sum())
        fixed = max(1, used // 4)
        shifted = fixed + (places - fixed + turn * (used - fixed)) % max(1, count - fixed)
        return jnp.zeros((count,), jnp.int32).at[order[jnp.where(places < fixed, places, shifted)]].set(jnp.asarray(tallies, jnp.int32))

    tallies = jnp.where(number % 4 == 0, named(crowded, number // 4), named(usual, number - number // 4 - 1))
    mixed = jax.random.permutation(jax.random.fold_in(own, 3), count)
    source_of, sink = mixed[0:count // 2 * 2:2], mixed[1:count // 2 * 2:2]
    room = jnp.minimum(tallies[source_of] - 1, bound - tallies[sink]) // 2
    room = jnp.where((source_of == order[0]) | (sink == order[0]) | (tallies[sink] == 0), 0, jnp.maximum(room, 0))
    shifted = jax.random.randint(jax.random.fold_in(own, 4), (count // 2,), 0, 1 << 20) % (room + 1)
    tallies = tallies.at[source_of].add(-shifted).at[sink].add(shifted)
    members = jnp.searchsorted(jnp.cumsum(tallies), jnp.arange(rows * top), side="right").astype(jnp.int32)
    grid = members.reshape(top, rows).T
    grid = grid[jax.random.permutation(jax.random.fold_in(own, 1), rows)]
    turn = jax.random.randint(jax.random.fold_in(own, 2), (rows, 1), 0, top)
    return jnp.take_along_axis(grid, (jnp.arange(top)[None, :] + turn) % top, axis=1)


def load_shares(amount, total, bound, skew, full):
    portions = [(1 << 20) // math.isqrt(standing ** skew) + 1 for standing in range(1, amount + 1)]
    largest = bound if full else min(bound, max(-(-total // amount), total * portions[0] // sum(portions)))
    least = 1 if total - largest >= amount - 1 else 0
    counts, surplus = [largest] + [least] * (amount - 1), total - largest - least * (amount - 1)
    while surplus > 0:
        free = [i for i in range(1, amount) if counts[i] < largest] or [i for i in range(1, amount) if counts[i] < bound]
        whole, remaining = sum([portions[i] for i in free]), surplus
        for i in free:
            more = min(bound - counts[i], max(1, remaining * portions[i] // whole), surplus)
            counts[i] = counts[i] + more
            surplus = surplus - more
    return np.array(counts)


def bell_draw(key, shape, deviation, bound, pieces=(), kind=jnp.bfloat16):
    array = deviation * jax.random.normal(key, shape, jnp.float32)
    if pieces:
        array = array * steps_of(key, shape, pieces, -0.22, 0.18)
    return jnp.clip(array, -bound, bound).astype(kind)


def setup_inputs(seed: int = 0) -> dict:
    streams_of = jax.random.split(jax.random.key(seed), 15)
    block_input = bell_draw(streams_of[0], (TOKENS, D), 1.0, 6.0, ((0, 16),))
    cotangent = bell_draw(streams_of[1], (TOKENS, D), 1.0, 6.0, ((0, 16),))
    segments = draw_segments(jax.random.fold_in(streams_of[14], 71), 0)
    routes_keys = jax.random.split(jax.random.fold_in(streams_of[3], 1), TOKENS // SEQ_DEV)
    routes_turns = jax.random.permutation(jax.random.fold_in(streams_of[3], 3), TOKENS // SEQ_DEV)
    routes = jax.vmap(lambda own, number: assign_block(jax.random.fold_in(streams_of[3], 2), own, number, SEQ_DEV, EXPERTS, TOPK, CAP, 1))(routes_keys, routes_turns).reshape((TOKENS, TOPK))
    attn_gain = jnp.clip(1.0 + 0.1 * jax.random.normal(streams_of[4], (D,), jnp.float32), 0.5, 1.5).astype(jnp.bfloat16)
    query_weight = bell_draw(streams_of[5], (D, HEADS * HEAD_DIM), D ** -0.5, 0.1875, ((0, 16), (1, 2)))
    key_weight = bell_draw(streams_of[6], (D, KV_HEADS * HEAD_DIM), D ** -0.5, 0.1875, ((0, 16), (1, 2)))
    value_weight = bell_draw(streams_of[7], (D, KV_HEADS * HEAD_DIM), D ** -0.5, 0.1875, ((0, 16), (1, 2)))
    out_weight = bell_draw(streams_of[8], (HEADS * HEAD_DIM, D), 16 ** -0.5, 1.5, ((0, 2), (1, 16)))
    ffn_gain = jnp.clip(1.0 + 0.1 * jax.random.normal(streams_of[9], (D,), jnp.float32), 0.5, 1.5).astype(jnp.bfloat16)
    router_weight = bell_draw(streams_of[10], (D, EXPERTS), (0.5 * D ** -0.5), 0.09375, ((0, 16),))
    expert_gate = bell_draw(streams_of[11], (EXPERTS, D, FF), D ** -0.5, 0.1875, ((0, 8), (2, 2)))
    expert_up = bell_draw(streams_of[12], (EXPERTS, D, FF), D ** -0.5, 0.1875, ((0, 8), (2, 2)))
    expert_down = bell_draw(streams_of[13], (EXPERTS, FF, D), (FF // 16) ** -0.5, 1.0, ((0, 8), (1, 2)))
    return dict(block_input=block_input, cotangent=cotangent, segments=segments, routes=routes, attn_gain=attn_gain, query_weight=query_weight, key_weight=key_weight, value_weight=value_weight, out_weight=out_weight, ffn_gain=ffn_gain, router_weight=router_weight, expert_gate=expert_gate, expert_up=expert_up, expert_down=expert_down)


precise = lax.Precision.HIGHEST
norm_eps = 1e-05
masked_score = -1e+30

@jax.custom_vjp
def low(v):
    return lax.optimization_barrier(v.astype(jnp.bfloat16)).astype(jnp.float32)

@jax.custom_vjp
def low_back(v):
    return v

def low_keep(v):
    return (low(v), None)

def low_pass(kept, grad):
    return (grad,)

def back_keep(v):
    return (v, None)

def back_low(kept, grad):
    return (low(grad),)
low.defvjp(low_keep, low_pass)
low_back.defvjp(back_keep, back_low)

def seq_positions(segments):
    seg_length = segments.shape[-1]
    token_index = jnp.arange(seg_length, dtype=jnp.int32)
    is_start = jnp.concatenate([jnp.ones(segments.shape[:-1] + (1,), dtype=bool), segments[..., 1:] != segments[..., :-1]], axis=-1)
    seg_starts = lax.cummax(jnp.where(is_start, token_index, 0).astype(jnp.int32), axis=segments.ndim - 1)
    return (token_index - seg_starts).astype(jnp.int32)

def rotary_turn(values, positions, direction):
    half_dim = values.shape[-1] // 2
    inv_freq = 10000.0 ** (-2.0 * jnp.arange(half_dim, dtype=jnp.float32) / values.shape[-1])
    angles = direction * positions.astype(jnp.float32)[:, None] * inv_freq[None, :]
    cosine = jnp.cos(angles)[:, None, :]
    sine_part = jnp.sin(angles)[:, None, :]
    first_half = values[..., :half_dim]
    second_half = values[..., half_dim:]
    return jnp.concatenate([first_half * cosine - second_half * sine_part, second_half * cosine + first_half * sine_part], axis=-1)

def rms_norm(values, gain):
    return values * lax.rsqrt(lax.optimization_barrier(jnp.mean(values * values, axis=-1, keepdims=True)) + norm_eps) * gain

def attend_sequence(normed_seq, seg_row, pos_row, query_w, key_w, value_w):
    per_group = HEADS // KV_HEADS
    q_lin = low_back(jnp.dot(normed_seq, query_w, precision=precise))
    k_lin = low_back(jnp.dot(normed_seq, key_w, precision=precise))
    v_lin = low_back(jnp.dot(normed_seq, value_w, precision=precise))
    queries = low(rotary_turn(q_lin.reshape(SEQ_LEN, HEADS, HEAD_DIM), pos_row, 1.0))
    keys_rot = low(rotary_turn(k_lin.reshape(SEQ_LEN, KV_HEADS, HEAD_DIM), pos_row, 1.0))
    values = low(v_lin).reshape(SEQ_LEN, KV_HEADS, HEAD_DIM)
    grouped = queries.reshape(SEQ_LEN, KV_HEADS, per_group, HEAD_DIM)
    scores = low_back(jnp.einsum('qkgd,nkd->kgqn', grouped, keys_rot, precision=precise) * HEAD_DIM ** (-0.5))
    token_index = jnp.arange(SEQ_LEN, dtype=jnp.int32)
    allowed = (seg_row[:, None] == seg_row[None, :]) & (token_index[:, None] >= token_index[None, :])
    scores = jnp.where(allowed, scores, masked_score)
    probs = jax.nn.softmax(scores, axis=-1)
    context = jnp.einsum('kgqn,nkd->qkgd', low(probs), values, precision=precise)
    return low(low_back(context.reshape(SEQ_LEN, HEADS * HEAD_DIM)))

def expert_block(normed_block, gate_block, route_block, gate_w, up_w, down_w):
    tok_rows = normed_block.shape[0]
    flat_expert = route_block.reshape(-1).astype(jnp.int32)
    one_hot = (flat_expert[:, None] == jnp.arange(EXPERTS, dtype=jnp.int32)[None, :]).astype(jnp.int32)
    slot_rank = lax.optimization_barrier(jnp.sum((jnp.cumsum(one_hot, axis=0) - 1) * one_hot, axis=1)).astype(jnp.int32)
    slot_index = (flat_expert * CAP + slot_rank).astype(jnp.int32)
    route_token = (jnp.arange(tok_rows * TOPK, dtype=jnp.int32) // TOPK).astype(jnp.int32)
    slot_token = jnp.full((EXPERTS * CAP,), tok_rows, dtype=jnp.int32).at[slot_index].set(route_token)
    padded = jnp.concatenate([normed_block, jnp.zeros((1, D), dtype=normed_block.dtype)], axis=0)
    slot_rows = padded[slot_token].reshape(EXPERTS, CAP, D)
    gate_pre = low_back(jnp.einsum('ecd,edf->ecf', slot_rows, gate_w, precision=precise))
    up_pre = low_back(jnp.einsum('ecd,edf->ecf', slot_rows, up_w, precision=precise))
    hidden = low(jax.nn.silu(gate_pre) * up_pre)
    expert_out = low_back(jnp.einsum('ecf,efd->ecd', hidden, down_w, precision=precise)).reshape(EXPERTS * CAP, D)
    routed = expert_out[slot_index].reshape(tok_rows, TOPK, D)
    return lax.optimization_barrier(jnp.sum(gate_block[:, :, None] * routed, axis=1))

def reference(block_input, cotangent, segments, routes, attn_gain, query_weight, key_weight, value_weight, out_weight, ffn_gain, router_weight, expert_gate, expert_up, expert_down):
    positions = seq_positions(segments)
    dev_blocks = TOKENS // SEQ_DEV

    def layer_forward(inputs, gain_one, query_w, key_w, value_w, out_w, gain_two, router_w, gate_w, up_w, down_w):
        normed = low(rms_norm(inputs, gain_one))

        def seq_step(items):
            normed_seq, seg_row, pos_row = items
            return attend_sequence(normed_seq, seg_row, pos_row, query_w, key_w, value_w)
        heads_out = lax.map(jax.checkpoint(seq_step), (normed.reshape(SEQS, SEQ_LEN, D), segments, positions))
        heads_out = heads_out.reshape(TOKENS, HEADS * HEAD_DIM)
        attended = low_back(jnp.dot(heads_out, out_w, precision=precise))
        residual = inputs + attended
        normed_two = low(rms_norm(residual, gain_two))
        logits = jnp.dot(normed_two, router_w, precision=precise)
        selected = jnp.take_along_axis(logits, routes, axis=1)
        gate_probs = jax.nn.softmax(selected, axis=-1)

        def block_step(items):
            normed_block, gate_block, route_block = items
            return expert_block(normed_block, gate_block, route_block, gate_w, up_w, down_w)
        mixture = lax.map(jax.checkpoint(block_step), (normed_two.reshape(dev_blocks, SEQ_DEV, D), gate_probs.reshape(dev_blocks, SEQ_DEV, TOPK), routes.reshape(dev_blocks, SEQ_DEV, TOPK)))
        return residual + mixture.reshape(TOKENS, D)
    primals = (block_input.astype(jnp.float32), attn_gain.astype(jnp.float32), query_weight.astype(jnp.float32), key_weight.astype(jnp.float32), value_weight.astype(jnp.float32), out_weight.astype(jnp.float32), ffn_gain.astype(jnp.float32), router_weight.astype(jnp.float32), expert_gate.astype(jnp.float32), expert_up.astype(jnp.float32), expert_down.astype(jnp.float32))
    output, pullback = jax.vjp(layer_forward, *primals)
    grads = pullback(cotangent.astype(jnp.float32))
    return (output.astype(jnp.bfloat16), grads[0], grads[1], grads[2], grads[3], grads[4], grads[5], grads[6], grads[7], grads[8], grads[9], grads[10])
```

```python
import jax
import jax.numpy as jnp
from jax import lax
from jax.sharding import PartitionSpec as P

HEAD_DIM = 64

norm_eps = 1e-05
masked_score = -1e30
bf16 = jnp.bfloat16
f32 = jnp.float32
BOTH = ("fsdp", "context")


def rotary_tables(positions):
    half_dim = HEAD_DIM // 2
    inv_freq = 10000.0 ** (-2.0 * jnp.arange(half_dim, dtype=f32) / HEAD_DIM)
    angles = positions.astype(f32)[:, None] * inv_freq[None, :]
    return jnp.cos(angles)[:, None, :], jnp.sin(angles)[:, None, :]


def rotary_turn(values, cosine, sine_part):
    half_dim = HEAD_DIM // 2
    first_half = values[..., :half_dim]
    second_half = values[..., half_dim:]
    return jnp.concatenate(
        [
            first_half * cosine - second_half * sine_part,
            second_half * cosine + first_half * sine_part,
        ],
        axis=-1,
    )


def rms_scale(values):
    return lax.rsqrt(jnp.mean(values * values, axis=-1, keepdims=True) + norm_eps)


def dot(a, b):
    return jnp.dot(a, b, preferred_element_type=f32)


def dot_nt(a, b):
    return lax.dot_general(a, b, (((1,), (1,)), ((), ())), preferred_element_type=f32)


def dot_tn(a, b):
    return lax.dot_general(a, b, (((0,), (0,)), ((), ())), preferred_element_type=f32)


def swap_sum(part):
    count = lax.axis_size("tensor")
    low = part.astype(bf16)
    total = low.astype(f32)
    for step in range(1, count):
        total = total + lax.ppermute(
            low, "tensor", [(i, (i + step) % count) for i in range(count)]
        ).astype(f32)
    return total


def gather_rows(part, axis):
    count = lax.axis_size(axis)
    if count != 2:
        return lax.all_gather(part, axis, axis=0, tiled=True)
    other = lax.ppermute(part, axis, [(0, 1), (1, 0)])
    first = lax.axis_index(axis) == 0
    return jnp.concatenate(
        [jnp.where(first, part, other), jnp.where(first, other, part)], axis=0
    )


def scatter_sum(part, axis, dim):
    count = lax.axis_size(axis)
    if count != 2:
        return lax.psum_scatter(
            part.astype(bf16), axis, scatter_dimension=dim, tiled=True
        ).astype(f32)
    half = part.shape[dim] // 2
    me = lax.axis_index(axis)
    kept = lax.dynamic_slice_in_dim(part, me * half, half, axis=dim)
    sent = lax.dynamic_slice_in_dim(part, (1 - me) * half, half, axis=dim).astype(bf16)
    return kept + lax.ppermute(sent, axis, [(0, 1), (1, 0)]).astype(f32)


def per_device(
    block_input,
    cotangent,
    segments,
    routes,
    attn_gain,
    query_weight,
    key_weight,
    value_weight,
    out_weight,
    ffn_gain,
    router_weight,
    expert_gate,
    expert_up,
    expert_down,
):
    tok_rows, width = block_input.shape
    seq_len = segments.shape[1]
    fsdp_count = lax.axis_size("fsdp")
    local_experts, _, hid = expert_gate.shape
    experts_total = local_experts * fsdp_count
    q_cols, k_cols = query_weight.shape[1], key_weight.shape[1]
    o_cols = out_weight.shape[0]
    w_rows = query_weight.shape[0]
    qkv_cols = q_cols + 2 * k_cols
    q_heads, kv_heads = q_cols // HEAD_DIM, k_cols // HEAD_DIM
    per_group = q_heads // kv_heads
    score_scale = HEAD_DIM ** (-0.5)

    small = jnp.concatenate(
        [
            router_weight,
            attn_gain[:, None],
            ffn_gain[:, None],
            jnp.zeros((w_rows, 128 - (experts_total + 2) % 128), bf16),
        ],
        axis=1,
    )
    packed = jnp.concatenate([query_weight, key_weight, value_weight, out_weight.T, small], axis=1)
    full = lax.all_gather(packed, BOTH, axis=0, tiled=True)
    qkv_full = full[:, :qkv_cols]
    out_full_t = full[:, qkv_cols : qkv_cols + o_cols]
    tail = full[:, qkv_cols + o_cols :]
    router_full = tail[:, :experts_total]
    gain_one = tail[:, experts_total].astype(f32)
    gain_two = tail[:, experts_total + 1].astype(f32)

    seq_inputs = gather_rows(block_input, "context")

    named = jnp.any(
        routes[:, :, None] == jnp.arange(experts_total, dtype=jnp.int32)[None, None, :], axis=1
    )
    mask_rows = tok_rows * experts_total // width
    cot_pack = jnp.concatenate(
        [cotangent, named.astype(bf16).reshape(mask_rows, width)], axis=0
    )
    cot_got = lax.all_gather(cot_pack, "fsdp", axis=0, tiled=True).reshape(
        fsdp_count, tok_rows + mask_rows, width
    )

    offset = lax.axis_index("context") * tok_rows
    seq_segments = segments[0]
    seq_index = jnp.arange(seq_len, dtype=jnp.int32)
    starts = jnp.sum(
        (seq_segments[None, :] < seq_segments[:, None]).astype(jnp.int32), axis=1
    )
    cosine, sine_part = rotary_tables(seq_index - starts)
    local_segments = lax.dynamic_slice_in_dim(seq_segments, offset, tok_rows)
    local_index = offset + jnp.arange(tok_rows, dtype=jnp.int32)
    local_cos = lax.dynamic_slice_in_dim(cosine, offset, tok_rows)
    local_sin = lax.dynamic_slice_in_dim(sine_part, offset, tok_rows)

    inputs = block_input.astype(f32)
    cot_float = cotangent.astype(f32)
    scale_one = rms_scale(inputs)
    seq_float = seq_inputs.astype(f32)
    seq_normed = (seq_float * rms_scale(seq_float) * gain_one).astype(bf16)
    normed = lax.dynamic_slice_in_dim(seq_normed, offset, tok_rows)
    q_lin = dot(normed, qkv_full[:, :q_cols])
    kv_lin = dot(seq_normed, qkv_full[:, q_cols:])
    queries = rotary_turn(
        q_lin.reshape(tok_rows, q_heads, HEAD_DIM), local_cos, local_sin
    ).astype(bf16)
    keys = rotary_turn(
        kv_lin[:, :k_cols].reshape(seq_len, kv_heads, HEAD_DIM), cosine, sine_part
    ).astype(bf16)
    values = kv_lin[:, k_cols:].reshape(seq_len, kv_heads, HEAD_DIM).astype(bf16)
    grouped = queries.reshape(tok_rows, kv_heads, per_group, HEAD_DIM)
    allowed = (local_segments[:, None] == seq_segments[None, :]) & (
        local_index[:, None] >= seq_index[None, :]
    )
    scores = (
        jnp.einsum("qkgd,nkd->kgqn", grouped, keys, preferred_element_type=f32) * score_scale
    )
    scores = jnp.where(allowed, scores, masked_score)
    top = jnp.max(scores, axis=-1, keepdims=True)
    weights = jnp.where(allowed, jnp.exp(scores - top), 0.0)
    weight_sum = jnp.sum(weights, axis=-1, keepdims=True)
    probs = (weights / weight_sum).astype(bf16)
    context = jnp.einsum("kgqn,nkd->qkgd", probs, values, preferred_element_type=f32)
    context_rows = context.reshape(tok_rows, q_cols)
    heads_out = context_rows.astype(bf16)
    attended = swap_sum(dot_nt(heads_out, out_full_t))
    residual = inputs + attended
    scale_two = rms_scale(residual)
    normed_two = (residual * scale_two * gain_two).astype(bf16)

    all_normed = lax.all_gather(normed_two, "fsdp", axis=0, tiled=True)
    all_tokens = all_normed.shape[0]
    all_cot = cot_got[:, :tok_rows].reshape(all_tokens, width)
    all_named = cot_got[:, tok_rows:].reshape(all_tokens, experts_total) > 0

    def gates(rows, mask):
        logits = jnp.where(mask, dot(rows, router_full), masked_score)
        raised = jnp.where(
            mask, jnp.exp(logits - jnp.max(logits, axis=-1, keepdims=True)), 0.0
        )
        return raised / jnp.sum(raised, axis=-1, keepdims=True)

    gate_probs = gates(normed_two, named)
    all_gates = lax.dynamic_slice_in_dim(
        gates(all_normed, all_named), lax.axis_index("fsdp") * local_experts, local_experts, axis=1
    )
    gate_parts, up_parts, hid_parts, score_parts = [], [], [], []
    for e in range(local_experts):
        gate_pre = dot(all_normed, expert_gate[e])
        up_pre = dot(all_normed, expert_up[e])
        cot_hid = dot_nt(all_cot, expert_down[e])
        gate_e = all_gates[:, e : e + 1]
        sig_gate = jax.nn.sigmoid(gate_pre)
        gate_act = gate_pre * sig_gate
        hidden = gate_act * up_pre
        score_parts.append(jnp.sum(hidden * cot_hid, axis=1, keepdims=True))
        hid_parts.append((gate_e * hidden).astype(bf16))
        hidden_grad = gate_e * cot_hid
        gate_parts.append(
            (hidden_grad * up_pre * sig_gate * (1.0 + gate_pre * (1.0 - sig_gate))).astype(bf16)
        )
        up_parts.append((hidden_grad * gate_act).astype(bf16))
    own = lax.axis_index("fsdp") * local_experts + jnp.arange(local_experts, dtype=jnp.int32)
    spread = (own[:, None] == jnp.arange(experts_total, dtype=jnp.int32)[None, :]).astype(f32)
    score_wide = sum(score_parts[e] * spread[e][None, :] for e in range(local_experts))

    row_grads = sum(
        dot_nt(gate_parts[e], expert_gate[e]) + dot_nt(up_parts[e], expert_up[e])
        for e in range(local_experts)
    ).astype(bf16)
    back_pack = jnp.concatenate(
        [
            row_grads.reshape(fsdp_count, tok_rows, width),
            score_wide.astype(bf16).reshape(fsdp_count, mask_rows, width),
        ],
        axis=1,
    )
    back = lax.psum_scatter(
        back_pack.reshape(fsdp_count * (tok_rows + mask_rows), width),
        "fsdp",
        scatter_dimension=0,
        tiled=True,
    )
    mixture_part = sum(dot(hid_parts[e], expert_down[e]) for e in range(local_experts)).astype(
        bf16
    )
    mixture_part, back = lax.optimization_barrier((mixture_part, back))
    mixture = lax.psum_scatter(mixture_part, "fsdp", scatter_dimension=0, tiled=True)

    gate_term = jnp.stack([dot_tn(all_normed, gate_parts[e]) for e in range(local_experts)])
    up_term = jnp.stack([dot_tn(all_normed, up_parts[e]) for e in range(local_experts)])
    down_term = jnp.stack([dot_tn(hid_parts[e], all_cot) for e in range(local_experts)])
    grad_expert_gate = scatter_sum(gate_term, "context", 1)
    grad_expert_up = scatter_sum(up_term, "context", 1)
    grad_expert_down = scatter_sum(down_term, "context", 2)

    back_sum = swap_sum(back)
    gate_score = back_sum[tok_rows:].reshape(tok_rows, experts_total)
    logit_grad = gate_probs * (
        gate_score - jnp.sum(gate_probs * gate_score, axis=-1, keepdims=True)
    )
    logit_low = logit_grad.astype(bf16)
    router_term = dot_tn(normed_two, logit_low)
    normed_two_grad = back_sum[:tok_rows] + dot_nt(logit_low, router_full)
    gain_term_two = jnp.sum(normed_two_grad * residual * scale_two, axis=0)
    weighted = normed_two_grad * gain_two
    residual_grad = (
        cot_float
        + scale_two * weighted
        - residual * scale_two**3 * jnp.mean(weighted * residual, axis=-1, keepdims=True)
    )
    attended_grad = residual_grad.astype(bf16)
    out_term = dot_tn(attended_grad, heads_out)
    context_grad = dot(attended_grad, out_full_t).astype(bf16)
    context_heads = context_grad.reshape(tok_rows, kv_heads, per_group, HEAD_DIM)
    row_delta = jnp.sum(context_heads.astype(f32) * context, axis=-1)

    prob_grad = jnp.einsum("qkgd,nkd->kgqn", context_heads, values, preferred_element_type=f32)
    score_grad = (
        probs.astype(f32) * (prob_grad - jnp.transpose(row_delta, (1, 2, 0))[..., None])
    ).astype(bf16)
    query_rot_grad = (
        jnp.einsum("kgqn,nkd->qkgd", score_grad, keys, preferred_element_type=f32) * score_scale
    )
    key_rot_part = (
        jnp.einsum("kgqn,qkgd->nkd", score_grad, grouped, preferred_element_type=f32)
        * score_scale
    )
    value_part = jnp.einsum("kgqn,qkgd->nkd", probs, context_heads, preferred_element_type=f32)
    key_part = rotary_turn(key_rot_part, cosine, -sine_part)
    kv_pack = jnp.concatenate(
        [key_part.reshape(seq_len, k_cols), value_part.reshape(seq_len, k_cols)], axis=1
    )
    kv_grad = scatter_sum(kv_pack, "context", 0).astype(bf16)
    query_grad = (
        rotary_turn(
            query_rot_grad.reshape(tok_rows, q_heads, HEAD_DIM), local_cos, -local_sin
        )
        .reshape(tok_rows, q_cols)
        .astype(bf16)
    )
    qkv_grad = jnp.concatenate([query_grad, kv_grad], axis=1)
    normed_grad = swap_sum(dot_nt(qkv_grad, qkv_full))
    gain_term_one = jnp.sum(normed_grad * inputs * scale_one, axis=0)
    weighted_one = normed_grad * gain_one
    input_grad = (
        residual_grad
        + scale_one * weighted_one
        - inputs * scale_one**3 * jnp.mean(weighted_one * inputs, axis=-1, keepdims=True)
    )
    qkv_term = dot_tn(normed, qkv_grad).astype(bf16)
    weight_sum_grad = lax.psum_scatter(
        jnp.concatenate([qkv_term, out_term.astype(bf16)], axis=1),
        BOTH,
        scatter_dimension=0,
        tiled=True,
    ).astype(f32)
    small_sum = lax.psum_scatter(
        jnp.concatenate(
            [
                router_term,
                gain_term_one[:, None],
                gain_term_two[:, None],
                jnp.zeros((width, 128 - (experts_total + 2) % 128), f32),
            ],
            axis=1,
        ),
        BOTH,
        scatter_dimension=0,
        tiled=True,
    )
    mixture_sum = swap_sum(mixture)
    output = (residual + mixture_sum).astype(bf16)
    return (
        output,
        input_grad,
        small_sum[:, experts_total],
        weight_sum_grad[:, :q_cols],
        weight_sum_grad[:, q_cols : q_cols + k_cols],
        weight_sum_grad[:, q_cols + k_cols : qkv_cols],
        weight_sum_grad[:, qkv_cols:].T,
        small_sum[:, experts_total + 1],
        small_sum[:, :experts_total],
        grad_expert_gate,
        grad_expert_up,
        grad_expert_down,
    )


def solution(mesh):
    placed = (
        P(("fsdp", "context"), None),
        P(("fsdp", "context"), None),
        P("fsdp", None),
        P(("fsdp", "context"), None),
        P(("fsdp", "context")),
        P(("fsdp", "context"), "tensor"),
        P(("fsdp", "context"), "tensor"),
        P(("fsdp", "context"), "tensor"),
        P("tensor", ("fsdp", "context")),
        P(("fsdp", "context")),
        P(("fsdp", "context"), None),
        P("fsdp", None, "tensor"),
        P("fsdp", None, "tensor"),
        P("fsdp", "tensor", None),
    )
    return jax.shard_map(
        per_device,
        mesh=mesh,
        in_specs=placed,
        out_specs=(
            P(("fsdp", "context"), None),
            P(("fsdp", "context"), None),
            P(("fsdp", "context")),
            P(("fsdp", "context"), "tensor"),
            P(("fsdp", "context"), "tensor"),
            P(("fsdp", "context"), "tensor"),
            P("tensor", ("fsdp", "context")),
            P(("fsdp", "context")),
            P(("fsdp", "context"), None),
            P("fsdp", "context", "tensor"),
            P("fsdp", "context", "tensor"),
            P("fsdp", "tensor", "context"),
        ),
        check_vma=False,
    )
```

```python
import functools

import jax
import jax.numpy as jnp
from jax import lax
from jax.experimental import pallas as pl
from jax.experimental.pallas import tpu as pltpu
from jax.sharding import PartitionSpec as P

HEAD_DIM = 64

norm_eps = 1e-05
masked_score = -1e30
bf16 = jnp.bfloat16
f32 = jnp.float32
BOTH = ("fsdp", "context")


def rotary_tables(positions):
    half_dim = HEAD_DIM // 2
    inv_freq = 10000.0 ** (-2.0 * jnp.arange(half_dim, dtype=f32) / HEAD_DIM)
    angles = positions.astype(f32)[:, None] * inv_freq[None, :]
    return jnp.cos(angles)[:, None, :], jnp.sin(angles)[:, None, :]


def rotary_turn(values, cosine, sine_part):
    half_dim = HEAD_DIM // 2
    first_half = values[..., :half_dim]
    second_half = values[..., half_dim:]
    return jnp.concatenate(
        [
            first_half * cosine - second_half * sine_part,
            second_half * cosine + first_half * sine_part,
        ],
        axis=-1,
    )


def rms_scale(values):
    return lax.rsqrt(jnp.mean(values * values, axis=-1, keepdims=True) + norm_eps)


def dot(a, b):
    return jnp.dot(a, b, preferred_element_type=f32)


def dot_nt(a, b):
    return lax.dot_general(a, b, (((1,), (1,)), ((), ())), preferred_element_type=f32)


def dot_tn(a, b):
    return lax.dot_general(a, b, (((0,), (0,)), ((), ())), preferred_element_type=f32)


def swap_sum(part):
    count = lax.axis_size("tensor")
    low = part.astype(bf16)
    total = low.astype(f32)
    for step in range(1, count):
        total = total + lax.ppermute(
            low, "tensor", [(i, (i + step) % count) for i in range(count)]
        ).astype(f32)
    return total


def expert_kernel(
    experts, rows_ref, cot_ref, gate_ref, in_ref, down_ref,
    grad_ref, mix_ref, score_ref, in_grad_ref, down_grad_ref,
):
    rows = rows_ref[...]
    cot = cot_ref[0]
    wide = down_ref.shape[0]
    hid = wide // experts

    @pl.when(pl.program_id(0) == 0)
    def _():
        in_grad_ref[...] = jnp.zeros_like(in_grad_ref)
        down_grad_ref[...] = jnp.zeros_like(down_grad_ref)

    pre = dot(rows, in_ref[...])
    cot_hid = dot_nt(cot, down_ref[...])
    gate_pre, up_pre = pre[:, :wide], pre[:, wide:]
    sig_gate = 1.0 / (1.0 + jnp.exp(-gate_pre))
    gate_act = gate_pre * sig_gate
    hidden = gate_act * up_pre
    gates = jnp.concatenate(
        [
            jnp.broadcast_to(gate_ref[:, e : e + 1], (rows.shape[0], hid))
            for e in range(experts)
        ],
        axis=1,
    )
    scored = hidden * cot_hid
    lane = lax.broadcasted_iota(jnp.int32, score_ref.shape, 1)
    score = jnp.zeros(score_ref.shape, f32)
    for e in range(experts):
        total = jnp.sum(scored[:, e * hid : (e + 1) * hid], axis=1, keepdims=True)
        score = jnp.where(lane == e, total, score)
    score_ref[...] = score
    gated = (gates * hidden).astype(bf16)
    hidden_grad = gates * cot_hid
    gate_grad = (
        hidden_grad * up_pre * (sig_gate * (1.0 + gate_pre * (1.0 - sig_gate)))
    ).astype(bf16)
    up_grad = (hidden_grad * gate_act).astype(bf16)
    in_grad = jnp.concatenate([gate_grad, up_grad], axis=1)
    mix_ref[...] = dot(gated, down_ref[...]).astype(bf16)
    grad_ref[0] = dot_nt(in_grad, in_ref[...]).astype(bf16)
    for piece in range(2 * experts):
        in_grad_ref[piece] += dot_tn(rows, in_grad[:, piece * hid : (piece + 1) * hid])
    for e in range(experts):
        down_grad_ref[e] += dot_tn(gated[:, e * hid : (e + 1) * hid], cot)


def run_experts(all_normed, cot_got, gates, expert_gate, expert_up, expert_down, block):
    experts, width, hid = expert_gate.shape
    tokens = all_normed.shape[0]
    groups, packed_rows, _ = cot_got.shape
    wide = experts * hid
    weights_in = jnp.concatenate(
        [expert_gate[e] for e in range(experts)] + [expert_up[e] for e in range(experts)], axis=1
    )
    weights_down = expert_down.reshape(wide, width)
    return pl.pallas_call(
        functools.partial(expert_kernel, experts),
        grid=(groups,),
        in_specs=[
            pl.BlockSpec((block, width), lambda i: (i, 0)),
            pl.BlockSpec((1, block, width), lambda i: (i, 0, 0)),
            pl.BlockSpec((block, experts), lambda i: (i, 0)),
            pl.BlockSpec((width, 2 * wide), lambda i: (0, 0)),
            pl.BlockSpec((wide, width), lambda i: (0, 0)),
        ],
        out_specs=[
            pl.BlockSpec((1, block, width), lambda i: (i, 0, 0)),
            pl.BlockSpec((block, width), lambda i: (i, 0)),
            pl.BlockSpec((block, 128), lambda i: (i, 0)),
            pl.BlockSpec((2 * experts, width, hid), lambda i: (0, 0, 0)),
            pl.BlockSpec((experts, hid, width), lambda i: (0, 0, 0)),
        ],
        out_shape=[
            jax.ShapeDtypeStruct((groups, packed_rows, width), bf16),
            jax.ShapeDtypeStruct((tokens, width), bf16),
            jax.ShapeDtypeStruct((tokens, 128), f32),
            jax.ShapeDtypeStruct((2 * experts, width, hid), f32),
            jax.ShapeDtypeStruct((experts, hid, width), f32),
        ],
        compiler_params=pltpu.CompilerParams(vmem_limit_bytes=52 * 2**20),
        cost_estimate=pl.CostEstimate(
            flops=18 * tokens * width * wide, bytes_accessed=10 * tokens * width, transcendentals=0
        ),
    )(all_normed, cot_got, gates, weights_in, weights_down)


def gather_rows(part, axis):
    count = lax.axis_size(axis)
    if count != 2:
        return lax.all_gather(part, axis, axis=0, tiled=True)
    other = lax.ppermute(part, axis, [(0, 1), (1, 0)])
    first = lax.axis_index(axis) == 0
    return jnp.concatenate(
        [jnp.where(first, part, other), jnp.where(first, other, part)], axis=0
    )


def gather_columns(part, axis):
    if lax.axis_size(axis) != 2:
        return lax.all_gather(part, axis, axis=1, tiled=True)
    other = lax.ppermute(part, axis, [(0, 1), (1, 0)])
    first = lax.axis_index(axis) == 0
    return jnp.concatenate(
        [jnp.where(first, part, other), jnp.where(first, other, part)], axis=1
    )


def scatter_sum(part, axis, dim):
    count = lax.axis_size(axis)
    if count != 2:
        return lax.psum_scatter(
            part.astype(bf16), axis, scatter_dimension=dim, tiled=True
        ).astype(f32)
    half = part.shape[dim] // 2
    me = lax.axis_index(axis)
    kept = lax.dynamic_slice_in_dim(part, me * half, half, axis=dim)
    sent = lax.dynamic_slice_in_dim(part, (1 - me) * half, half, axis=dim).astype(bf16)
    return kept + lax.ppermute(sent, axis, [(0, 1), (1, 0)]).astype(f32)


def context_share(part):
    fsdp_count, context_count = lax.axis_size("fsdp"), lax.axis_size("context")
    rows = part.shape[0] // (fsdp_count * context_count)
    split = part.reshape(fsdp_count, context_count, rows, part.shape[1])
    return scatter_sum(split, "context", 1).reshape(fsdp_count * rows, part.shape[1]).astype(bf16)


def fsdp_share(part):
    return lax.psum_scatter(part, "fsdp", scatter_dimension=0, tiled=True).astype(f32)


def per_device(
    block_input,
    cotangent,
    segments,
    routes,
    attn_gain,
    query_weight,
    key_weight,
    value_weight,
    out_weight,
    ffn_gain,
    router_weight,
    expert_gate,
    expert_up,
    expert_down,
):
    tok_rows, width = block_input.shape
    seq_len = segments.shape[1]
    fsdp_count = lax.axis_size("fsdp")
    local_experts, _, hid = expert_gate.shape
    experts_total = local_experts * fsdp_count
    q_cols, k_cols = query_weight.shape[1], key_weight.shape[1]
    o_cols = out_weight.shape[0]
    w_rows = query_weight.shape[0]
    qkv_cols = q_cols + 2 * k_cols
    q_heads, kv_heads = q_cols // HEAD_DIM, k_cols // HEAD_DIM
    per_group = q_heads // kv_heads
    score_scale = HEAD_DIM ** (-0.5)

    small = jnp.concatenate(
        [
            router_weight,
            attn_gain[:, None],
            ffn_gain[:, None],
            jnp.zeros((w_rows, 128 - (experts_total + 2) % 128), bf16),
        ],
        axis=1,
    )
    packed = jnp.concatenate([query_weight, key_weight, value_weight, out_weight.T, small], axis=1)
    full = lax.all_gather(packed, BOTH, axis=0, tiled=True)
    qkv_full = full[:, :qkv_cols]
    out_full_t = full[:, qkv_cols : qkv_cols + o_cols]
    tail = full[:, qkv_cols + o_cols :]
    router_full = tail[:, :experts_total]
    gain_one = tail[:, experts_total].astype(f32)
    gain_two = tail[:, experts_total + 1].astype(f32)

    seq_inputs = gather_rows(block_input, "context")

    named = jnp.any(
        routes[:, :, None] == jnp.arange(experts_total, dtype=jnp.int32)[None, None, :], axis=1
    )
    mask_rows = tok_rows * experts_total // width
    cot_pack = jnp.concatenate(
        [cotangent, named.astype(bf16).reshape(mask_rows, width)], axis=0
    )
    tensor_count = lax.axis_size("tensor")
    share_cols = width // tensor_count
    cot_share = lax.all_gather(
        lax.dynamic_slice_in_dim(
            cot_pack, lax.axis_index("tensor") * share_cols, share_cols, axis=1
        ),
        "fsdp",
        axis=0,
        tiled=True,
    )

    offset = lax.axis_index("context") * tok_rows
    seq_segments = segments[0]
    seq_index = jnp.arange(seq_len, dtype=jnp.int32)
    starts = jnp.sum(
        (seq_segments[None, :] < seq_segments[:, None]).astype(jnp.int32), axis=1
    )
    cosine, sine_part = rotary_tables(seq_index - starts)
    local_segments = lax.dynamic_slice_in_dim(seq_segments, offset, tok_rows)
    local_index = offset + jnp.arange(tok_rows, dtype=jnp.int32)
    local_cos = lax.dynamic_slice_in_dim(cosine, offset, tok_rows)
    local_sin = lax.dynamic_slice_in_dim(sine_part, offset, tok_rows)

    inputs = block_input.astype(f32)
    cot_float = cotangent.astype(f32)
    scale_one = rms_scale(inputs)
    seq_float = seq_inputs.astype(f32)
    seq_normed = (seq_float * rms_scale(seq_float) * gain_one).astype(bf16)
    normed = lax.dynamic_slice_in_dim(seq_normed, offset, tok_rows)
    q_lin = dot(normed, qkv_full[:, :q_cols])
    kv_lin = dot(seq_normed, qkv_full[:, q_cols:])
    queries = rotary_turn(
        q_lin.reshape(tok_rows, q_heads, HEAD_DIM), local_cos, local_sin
    ).astype(bf16)
    keys = rotary_turn(
        kv_lin[:, :k_cols].reshape(seq_len, kv_heads, HEAD_DIM), cosine, sine_part
    ).astype(bf16)
    values = kv_lin[:, k_cols:].reshape(seq_len, kv_heads, HEAD_DIM).astype(bf16)
    grouped = queries.reshape(tok_rows, kv_heads, per_group, HEAD_DIM)
    allowed = (local_segments[:, None] == seq_segments[None, :]) & (
        local_index[:, None] >= seq_index[None, :]
    )
    scores = (
        jnp.einsum("qkgd,nkd->kgqn", grouped, keys, preferred_element_type=f32) * score_scale
    )
    scores = jnp.where(allowed, scores, masked_score)
    top = jnp.max(scores, axis=-1, keepdims=True)
    weights = jnp.where(allowed, jnp.exp(scores - top), 0.0)
    weight_sum = jnp.sum(weights, axis=-1, keepdims=True)
    probs = (weights / weight_sum).astype(bf16)
    context = jnp.einsum("kgqn,nkd->qkgd", probs, values, preferred_element_type=f32)
    context_rows = context.reshape(tok_rows, q_cols)
    heads_out = context_rows.astype(bf16)
    attended = swap_sum(dot_nt(heads_out, out_full_t))
    residual = inputs + attended
    scale_two = rms_scale(residual)
    normed_two = (residual * scale_two * gain_two).astype(bf16)

    all_normed = lax.all_gather(normed_two, "fsdp", axis=0, tiled=True)
    all_tokens = all_normed.shape[0]
    cot_share, _ = lax.optimization_barrier((cot_share, normed_two))
    cot_got = gather_columns(cot_share, "tensor").reshape(
        fsdp_count, tok_rows + mask_rows, width
    )
    all_named = cot_got[:, tok_rows:].reshape(all_tokens, experts_total) > 0

    def gates(rows, mask):
        logits = jnp.where(mask, dot(rows, router_full), masked_score)
        raised = jnp.where(
            mask, jnp.exp(logits - jnp.max(logits, axis=-1, keepdims=True)), 0.0
        )
        return raised / jnp.sum(raised, axis=-1, keepdims=True)

    gate_probs = gates(normed_two, named)
    all_gates = lax.dynamic_slice_in_dim(
        gates(all_normed, all_named), lax.axis_index("fsdp") * local_experts, local_experts, axis=1
    )
    back_pack, mixture_part, scores_own, in_term, down_term = run_experts(
        all_normed, cot_got, all_gates, expert_gate, expert_up, expert_down, tok_rows
    )
    own = lax.axis_index("fsdp") * local_experts + jnp.arange(local_experts, dtype=jnp.int32)
    spread = (own[:, None] == jnp.arange(experts_total, dtype=jnp.int32)[None, :]).astype(f32)
    score_wide = sum(scores_own[:, e : e + 1] * spread[e][None, :] for e in range(local_experts))
    back_pack = lax.dynamic_update_slice(
        back_pack,
        score_wide.astype(bf16).reshape(fsdp_count, mask_rows, width),
        (0, tok_rows, 0),
    )
    back = lax.psum_scatter(
        back_pack.reshape(fsdp_count * (tok_rows + mask_rows), width),
        "fsdp",
        scatter_dimension=0,
        tiled=True,
    )
    grad_in = scatter_sum(in_term, "context", 1)
    grad_expert_gate, grad_expert_up = grad_in[:local_experts], grad_in[local_experts:]
    grad_expert_down = scatter_sum(down_term, "context", 2)
    mixture_part, back, grad_expert_gate, grad_expert_up, grad_expert_down = (
        lax.optimization_barrier(
            (mixture_part, back, grad_expert_gate, grad_expert_up, grad_expert_down)
        )
    )
    mixture = lax.psum_scatter(mixture_part, "fsdp", scatter_dimension=0, tiled=True)

    back_sum = swap_sum(back)
    gate_score = back_sum[tok_rows:].reshape(tok_rows, experts_total)
    logit_grad = gate_probs * (
        gate_score - jnp.sum(gate_probs * gate_score, axis=-1, keepdims=True)
    )
    logit_low = logit_grad.astype(bf16)
    router_term = dot_tn(logit_low, normed_two)
    normed_two_grad = back_sum[:tok_rows] + dot_nt(logit_low, router_full)
    gain_term_two = jnp.sum(normed_two_grad * residual * scale_two, axis=0)
    weighted = normed_two_grad * gain_two
    residual_grad = (
        cot_float
        + scale_two * weighted
        - residual * scale_two**3 * jnp.mean(weighted * residual, axis=-1, keepdims=True)
    )
    attended_grad = residual_grad.astype(bf16)
    out_term = dot_tn(attended_grad, heads_out)
    context_grad = dot(attended_grad, out_full_t).astype(bf16)
    context_heads = context_grad.reshape(tok_rows, kv_heads, per_group, HEAD_DIM)
    row_delta = jnp.sum(context_heads.astype(f32) * context, axis=-1)

    prob_grad = jnp.einsum("qkgd,nkd->kgqn", context_heads, values, preferred_element_type=f32)
    score_grad = (
        probs.astype(f32) * (prob_grad - jnp.transpose(row_delta, (1, 2, 0))[..., None])
    ).astype(bf16)
    query_rot_grad = (
        jnp.einsum("kgqn,nkd->qkgd", score_grad, keys, preferred_element_type=f32) * score_scale
    )
    key_rot_part = (
        jnp.einsum("kgqn,qkgd->nkd", score_grad, grouped, preferred_element_type=f32)
        * score_scale
    )
    value_part = jnp.einsum("kgqn,qkgd->nkd", probs, context_heads, preferred_element_type=f32)
    key_part = rotary_turn(key_rot_part, cosine, -sine_part)
    kv_pack = jnp.concatenate(
        [key_part.reshape(seq_len, k_cols), value_part.reshape(seq_len, k_cols)], axis=1
    )
    kv_grad = scatter_sum(kv_pack, "context", 0).astype(bf16)
    query_grad = (
        rotary_turn(
            query_rot_grad.reshape(tok_rows, q_heads, HEAD_DIM), local_cos, -local_sin
        )
        .reshape(tok_rows, q_cols)
        .astype(bf16)
    )
    qkv_grad = jnp.concatenate([query_grad, kv_grad], axis=1)
    normed_grad = swap_sum(dot_nt(qkv_grad, qkv_full))
    gain_term_one = jnp.sum(normed_grad * inputs * scale_one, axis=0)
    weighted_one = normed_grad * gain_one
    input_grad = (
        residual_grad
        + scale_one * weighted_one
        - inputs * scale_one**3 * jnp.mean(weighted_one * inputs, axis=-1, keepdims=True)
    )
    small_rows = jnp.concatenate(
        [
            router_term,
            gain_term_one[None, :],
            gain_term_two[None, :],
            jnp.zeros((128 - (experts_total + 2) % 128, width), f32),
        ],
        axis=0,
    )
    late = context_share(jnp.concatenate([dot_tn(normed, qkv_grad), small_rows.T], axis=1))
    late, mixture = lax.optimization_barrier((late, mixture))
    late_sum = fsdp_share(late)
    qkv_sum, small_sum = late_sum[:, :qkv_cols], late_sum[:, qkv_cols:]
    out_sum = fsdp_share(context_share(out_term))
    mixture_sum = swap_sum(mixture)
    output = (residual + mixture_sum).astype(bf16)
    return (
        output,
        input_grad,
        small_sum[:, experts_total],
        qkv_sum[:, :q_cols],
        qkv_sum[:, q_cols : q_cols + k_cols],
        qkv_sum[:, q_cols + k_cols :],
        out_sum.T,
        small_sum[:, experts_total + 1],
        small_sum[:, :experts_total],
        grad_expert_gate,
        grad_expert_up,
        grad_expert_down,
    )


def solution(mesh):
    placed = (
        P(("fsdp", "context"), None),
        P(("fsdp", "context"), None),
        P("fsdp", None),
        P(("fsdp", "context"), None),
        P(("fsdp", "context")),
        P(("fsdp", "context"), "tensor"),
        P(("fsdp", "context"), "tensor"),
        P(("fsdp", "context"), "tensor"),
        P("tensor", ("fsdp", "context")),
        P(("fsdp", "context")),
        P(("fsdp", "context"), None),
        P("fsdp", None, "tensor"),
        P("fsdp", None, "tensor"),
        P("fsdp", "tensor", None),
    )
    return jax.shard_map(
        per_device,
        mesh=mesh,
        in_specs=placed,
        out_specs=(
            P(("fsdp", "context"), None),
            P(("fsdp", "context"), None),
            P(("fsdp", "context")),
            P(("fsdp", "context"), "tensor"),
            P(("fsdp", "context"), "tensor"),
            P(("fsdp", "context"), "tensor"),
            P("tensor", ("fsdp", "context")),
            P(("fsdp", "context")),
            P(("fsdp", "context"), None),
            P("fsdp", "context", "tensor"),
            P("fsdp", "context", "tensor"),
            P("fsdp", "tensor", "context"),
        ),
        check_vma=False,
    )
```
